512 devices in a mesh: dp: 8 (over z_hi, core), frame: 64 (over z_lo, y, x).
Axes of the slice: x: 4, y: 4, z: 16 (z_hi: 4, z_lo: 4; z = z_hi * 4 + z_lo), core: 2. Of those that a mesh axis runs over, the one named last changes fastest.
Arguments:
- queries: bfloat16 [262144, 576], P(('dp', 'frame')), may hold values from -6 to 6
- key_vectors: bfloat16 [262144, 576], P(('dp', 'frame')), may hold values from -6 to 6
- values: bfloat16 [262144, 576], P(('dp', 'frame')), may hold values from -6 to 6
- w_out: bfloat16 [576, 1152], P('frame'), may hold values from -0.25 to 0.25
- cotangent: bfloat16 [262144, 1152], P(('dp', 'frame')), may hold values from -24 to 24
Outputs:
- query_grad: bfloat16 [262144, 576], P(('dp', 'frame'))
- key_grad: bfloat16 [262144, 576], P(('dp', 'frame'))
- value_grad: bfloat16 [262144, 576], P(('dp', 'frame'))
- w_grad: bfloat16 [576, 1152], P('frame')
The draws below stay inside these ranges and needn't reach their ends.
All inputs are finite; a program needn't handle non-finite values.
Results may differ from the reference program's by a relative error of at most 0.012.
Values may be sent and summed in bfloat16 or wider, within the bound.
A program may use at most 64 MiB of HBM per device.

```python
import math
import jax
import jax.numpy as jnp
from jax import lax

D = 1152
HS = 72
HEADS = 8
PT = 256
CLIPS = 2
HW = 576
FRAMES = 64
TOKENS = 262144
N_DP = 8


def draw_queries(key, part):
    key = jax.random.fold_in(key, 41)
    base = jax.random.truncated_normal(key, -4.0, 4.0, (TOKENS, HEADS * HS), jnp.float32)
    return base.astype(jnp.bfloat16)


def draw_key_vectors(key, part):
    key = jax.random.fold_in(key, 42)
    base = jax.random.truncated_normal(key, -4.0, 4.0, (TOKENS, HEADS * HS), jnp.float32)
    return base.astype(jnp.bfloat16)


def spiked(entries, stream_key, source, target, parts, factor):
    owner, partner = [(jnp.arange(entries.shape[dim]) // (entries.shape[dim] // parts)).reshape([-1 if axis == dim else 1 for axis in range(entries.ndim)]) for dim in (source, target)]
    chosen = jax.random.permutation(stream_key, parts)[partner]
    strong = (owner == chosen) | (owner == (partner + parts // 2) % parts)
    return jnp.where(strong, factor * entries, entries)


def block_scale(key, shape, split, smallest, top_value):
    def one(axis_at, blocks):
        heights = jax.random.uniform(jax.random.fold_in(jax.random.fold_in(key, 6), axis_at), (blocks,), jnp.float32, smallest / len(split), top_value / len(split))
        return jnp.repeat(jnp.exp(heights), shape[axis_at] // blocks).reshape((-1,) + (1,) * (len(shape) - axis_at - 1))

    gain = one(*split[0])
    for cut in split[1:]:
        gain = gain * one(*cut)
    return gain


def noise(stream_key, shape, deviation, reach, split=(), kind=jnp.bfloat16):
    drawn = deviation * jax.random.normal(stream_key, shape, jnp.float32)
    if split:
        drawn = drawn * block_scale(stream_key, shape, split, -0.22, 0.18)
    return jnp.clip(drawn, -reach, reach).astype(kind)


def gaussian_with(stream_key, extent, width, limit, shards, heavy, kind=jnp.bfloat16):
    values = width * jax.random.normal(stream_key, extent, jnp.float32)
    if shards:
        values = values * block_scale(stream_key, extent, shards, -0.22, 0.18)
    return jnp.clip(spiked(values, jax.random.fold_in(stream_key, 3), *heavy), -limit, limit).astype(kind)


def setup_inputs(seed: int = 0) -> dict:
    seeds = jax.random.split(jax.random.key(seed), 6)
    queries = draw_queries(jax.random.fold_in(seeds[5], 71), 0)
    key_vectors = draw_key_vectors(jax.random.fold_in(seeds[5], 71), 0)
    values = noise(seeds[2], (TOKENS, HW), 1.0, 6.0, ((0, 512),))
    w_out = noise(seeds[3], (HW, D), HW ** -0.5, 0.25, ((0, 64),))
    cotangent = gaussian_with(seeds[4], (TOKENS, D), 1.0, 24.0, ((0, 512),), (0, 1, 128, 5.5))
    return {"queries": queries, "key_vectors": key_vectors, "values": values, "w_out": w_out, "cotangent": cotangent}


def widen(array):
    return array.astype(jnp.float32)

def rounded(array):
    return lax.optimization_barrier(array.astype(jnp.bfloat16)).astype(jnp.float32)

def attend_forward(queries, key_vectors, values, softmax_scale):
    scores = jnp.einsum('blhs,bmhs->bhlm', widen(queries), widen(key_vectors)) * softmax_scale
    probabilities = jax.nn.softmax(scores, axis=-1)
    mixture = jnp.einsum('bhlm,bmhs->blhs', rounded(probabilities), widen(values))
    return mixture.astype(jnp.bfloat16)

def attend_backward(queries, key_vectors, values, upstream, softmax_scale):
    scores = jnp.einsum('blhs,bmhs->bhlm', widen(queries), widen(key_vectors)) * softmax_scale
    probabilities = jax.nn.softmax(scores, axis=-1)
    weights_low = rounded(probabilities)
    grad_probs = jnp.einsum('blhs,bmhs->bhlm', widen(upstream), widen(values))
    value_grad = jnp.einsum('bhlm,blhs->bmhs', weights_low, widen(upstream)).astype(jnp.bfloat16)
    row_inner = lax.optimization_barrier(jnp.sum(probabilities * grad_probs, axis=-1, keepdims=True))
    grad_scores = rounded(probabilities * (grad_probs - row_inner))
    query_grad = (jnp.einsum('bhlm,bmhs->blhs', grad_scores, widen(key_vectors)) * softmax_scale).astype(jnp.bfloat16)
    key_grad = (jnp.einsum('bhlm,blhs->bmhs', grad_scores, widen(queries)) * softmax_scale).astype(jnp.bfloat16)
    return (query_grad, key_grad, value_grad)

def reference(queries, key_vectors, values, w_out, cotangent):
    half_heads = HEADS // 2
    softmax_scale = 1.0 / math.sqrt(HS)
    full_shape = (N_DP, FRAMES, CLIPS, PT, HEADS, HS)

    def spatial_split(array):
        return array.reshape(full_shape)[..., :half_heads, :].reshape(N_DP * FRAMES, CLIPS, PT, half_heads, HS)

    def temporal_split(array):
        part_view = array.reshape(full_shape)[..., half_heads:, :]
        return jnp.transpose(part_view, (0, 2, 3, 1, 4, 5)).reshape(N_DP * CLIPS, PT, FRAMES, half_heads, HS)

    def combine(spatial_part, temporal_part):
        spatial_full = spatial_part.reshape(N_DP, FRAMES, CLIPS, PT, half_heads, HS)
        temporal_full = jnp.transpose(temporal_part.reshape(N_DP, CLIPS, PT, FRAMES, half_heads, HS), (0, 3, 1, 2, 4, 5))
        return jnp.concatenate([spatial_full, temporal_full], axis=4).reshape(TOKENS, HEADS * HS)

    def forward_one(group):
        return attend_forward(group[0], group[1], group[2], softmax_scale)

    def backward_one(group):
        return attend_backward(group[0], group[1], group[2], group[3], softmax_scale)
    spatial_out = lax.map(forward_one, (spatial_split(queries), spatial_split(key_vectors), spatial_split(values)))
    temporal_out = lax.map(forward_one, (temporal_split(queries), temporal_split(key_vectors), temporal_split(values)))
    attended = combine(spatial_out, temporal_out)
    summed = jnp.dot(attended.T, cotangent, preferred_element_type=jnp.float32)
    w_grad = (summed * (1.0 / math.sqrt(TOKENS))).astype(jnp.bfloat16)
    upstream = jnp.dot(cotangent, w_out.T, preferred_element_type=jnp.float32).astype(jnp.bfloat16)
    spatial_grads = lax.map(backward_one, (spatial_split(queries), spatial_split(key_vectors), spatial_split(values), spatial_split(upstream)))
    temporal_grads = lax.map(backward_one, (temporal_split(queries), temporal_split(key_vectors), temporal_split(values), temporal_split(upstream)))
    query_grad = combine(spatial_grads[0], temporal_grads[0])
    key_grad = combine(spatial_grads[1], temporal_grads[1])
    value_grad = combine(spatial_grads[2], temporal_grads[2])
    return (query_grad, key_grad, value_grad, w_grad)
```

```python
import math

import jax
import jax.numpy as jnp
import numpy as np
from jax import lax
from jax.experimental import pallas as pl
from jax.experimental.pallas import tpu as pltpu
from jax.sharding import PartitionSpec as P

HS = 72
HEADS = 8
PT = 256
D = 1152
HW = 576
ROWS = 512
SIDE = 288
PAIR = 144
MSG = 640
CUT = 384
BACK = 256
WIN = 640
OFF = 512
SHARE = 9
F = 64
MESH = pl.DeviceIdType.MESH
BF = jnp.bfloat16
F32 = jnp.float32

(W_Z, W_Y, W_X, W_C, SEND_A, SEND_B, BACK_A, BACK_B, G_C0, G_X0, G_Y0, G_C1, G_X1, G_Y1, G_Z, G_H, G_F, OWN) = range(18)
STAGES = 18


def group_rows():
    m = np.zeros((256, 256), np.float32)
    for g in range(4):
        for f in range(16):
            for s in range(4):
                m[64 * g + 4 * f + s, 16 * f + 4 * g + s] = 1
    return m


def w_after_z():
    m = np.zeros((48, 64), np.float32)
    for z in range(4):
        for i in range(SHARE):
            m[z * SHARE + i, z * 16 + i] = 1
    return m


def w_after_y():
    m = np.zeros((144, 192), np.float32)
    for y in range(4):
        for r in range(36):
            m[y * 36 + r, y * 48 + r] = 1
    return m


def upstream_columns():
    m = np.zeros((HW, HW), np.float32)
    for x in range(4):
        for y in range(4):
            for z in range(4):
                for i in range(SHARE):
                    m[x * 144 + y * 36 + z * 9 + i, (z * 16 + y * 4 + x) * 9 + i] = 1
    return m


def attended_columns():
    m = np.zeros((SIDE, 320), np.float32)
    for x in range(4):
        for y in range(4):
            for zz in range(2):
                for i in range(SHARE):
                    m[(zz * 16 + y * 4 + x) * 9 + i, x * 80 + y * 18 + zz * 9 + i] = 1
    return m


def grad_after_x():
    m = np.zeros((128, 80), np.float32)
    for y in range(4):
        for r in range(18):
            m[y * 32 + r, y * 18 + r] = 1
    return m


def grad_after_y():
    m = np.zeros((64, 64), np.float32)
    for h in range(2):
        for zz in range(2):
            for i in range(SHARE):
                m[(2 * h + zz) * 16 + i, h * 32 + zz * 9 + i] = 1
    return m


def dot(a, b, ca, cb):
    return lax.dot_general(a, b, (((ca,), (cb,)), ((), ())), preferred_element_type=F32)


def move(m, a):
    return dot(m, a, 1, 0).astype(BF)


def probs_of(q, k, scale, keep):
    s = dot(k, q, 1, 1) * scale
    if keep is not None:
        s = jnp.where(keep, s, -1e30)
    e = jnp.exp(s - jnp.max(s, axis=0, keepdims=True))
    return e / jnp.sum(e, axis=0, keepdims=True)


def attend(p, q, k, v, u, scale):
    p16 = p.astype(BF)
    att = dot(p16, v, 0, 0).astype(BF)
    dv = dot(p16, u, 1, 0).astype(BF)
    dp = dot(v, u, 1, 1)
    ds = (p * (dp - jnp.sum(p * dp, axis=0, keepdims=True))).astype(BF)
    dk = (dot(ds, q, 1, 0) * scale).astype(BF)
    dq = (dot(ds, k, 0, 0) * scale).astype(BF)
    return att, dv, dq, dk


def kernel(
    q_ref, k_ref, v_ref, w_ref, cot_ref,
    rows_m, wz_m, wy_m, up_m, att_m, gx_m, gy_m,
    dq_ref, dk_ref, dv_ref, wg_ref,
    wpad, g1, c1, g2, c2, wall, up, msg, got, grp, prob, res, out_msg, back,
    att, part, rc, xs, rx, ys, ry, zs, zp, rz, rh, fw,
    send, recv,
):
    me, d = lax.axis_index("frame"), lax.axis_index("dp")
    core, zhi = lax.rem(d, 2), lax.div(d, 2)
    x, y, z = lax.rem(me, 4), lax.rem(lax.div(me, 4), 4), lax.div(me, 16)
    scale = 1.0 / math.sqrt(HS)
    win = pl.multiple_of(core * OFF, 128)
    other_win = pl.multiple_of((1 - core) * OFF, 128)
    give = pl.multiple_of(core * WIN, 128)

    def rows16(i, n=16):
        return pl.ds(pl.multiple_of(i * n, 16), n)

    def frame(p):
        return {"frame": p}

    def on_x(i):
        return frame(me - x + lax.rem(x + i, 4))

    def on_y(i):
        return frame(me + 4 * (lax.rem(y + i, 4) - y))

    def on_z(i):
        return frame(me + 16 * (lax.rem(z + i, 4) - z))

    def on_zhi(i):
        return {"dp": lax.rem(d + 2 * i, 8)}

    sibling = {"dp": d + 1 - 2 * core}

    def put(src, dst, stage, to):
        pltpu.make_async_remote_copy(
            src_ref=src, dst_ref=dst, send_sem=send.at[stage], recv_sem=recv.at[stage],
            device_id=to, device_id_type=MESH,
        ).start()

    def arrived(ref, stage):
        pltpu.make_async_copy(ref, ref, recv.at[stage]).wait()

    def sent(ref, stage):
        pltpu.make_async_copy(ref, ref, send.at[stage]).wait()

    barrier = pltpu.get_barrier_semaphore()

    def greet(i, c):
        pl.semaphore_signal(barrier, inc=1, device_id=frame(lax.rem(me + i, F)), device_id_type=MESH)
        return c

    lax.fori_loop(1, F, greet, 0)
    for i in range(1, 4):
        pl.semaphore_signal(barrier, inc=1, device_id=on_zhi(i), device_id_type=MESH)
    pl.semaphore_signal(barrier, inc=1, device_id=sibling, device_id_type=MESH)

    wpad[...] = jnp.zeros_like(wpad)
    wpad[0:SHARE, :] = w_ref[:, pl.ds(win, WIN)]
    msg[:, :, HW:MSG] = jnp.zeros((2, ROWS, MSG - HW), BF)
    for hp in range(2):
        cols = slice(SIDE + PAIR * hp, SIDE + PAIR * (hp + 1))
        msg[hp, :, 0:PAIR] = q_ref[:, cols]
        msg[hp, :, PAIR : 2 * PAIR] = k_ref[:, cols]
        msg[hp, :, 2 * PAIR : 3 * PAIR] = v_ref[:, cols]

    pl.semaphore_wait(barrier, F - 1 + 4)

    for i in range(1, 4):
        put(wpad, g1.at[rows16(z)], W_Z, on_z(i))
    g1[rows16(z), :] = wpad[...]

    def send_messages(lo, hi, stage, first, last):
        def body(i, c):
            p = lax.rem(me + i, F)
            put(
                msg.at[lax.rem(p, 2), rows16(lax.div(p, 2)), lo:hi],
                got.at[rows16(me), lo:hi],
                stage,
                frame(p),
            )
            return c

        lax.fori_loop(first, last, body, 0)

    send_messages(0, CUT, SEND_A, 1, 22)
    arrived(g1.at[0:48], W_Z)
    c1[...] = move(wz_m[...], g1[...])
    for i in range(1, 4):
        put(c1, g2.at[rows16(y, 48)], W_Y, on_y(i))
    g2[rows16(y, 48), :] = c1[...]
    send_messages(0, CUT, SEND_A, 22, 43)
    arrived(g2.at[0:144], W_Y)
    c2[...] = move(wy_m[...], g2[...])
    for i in range(1, 4):
        put(c2, wall.at[rows16(x, 144), pl.ds(win, WIN)], W_X, on_x(i))
    wall[rows16(x, 144), pl.ds(win, WIN)] = c2[...]
    send_messages(0, CUT, SEND_A, 43, F)
    arrived(wall.at[0:432, 0:WIN], W_X)
    put(wall.at[:, pl.ds(give, OFF)], wall.at[:, pl.ds(give, OFF)], W_C, sibling)
    arrived(wall.at[:, 0:OFF], W_C)

    for r in range(2):
        here = slice(256 * r, 256 * (r + 1))
        u = dot(cot_ref[here, :], wall[...], 1, 1).astype(BF)
        u = dot(u, up_m[...], 1, 0).astype(BF)
        up[here, :] = u
        for hp in range(2):
            msg[hp, here, 3 * PAIR : HW] = u[:, SIDE + PAIR * hp : SIDE + PAIR * (hp + 1)]
    send_messages(CUT, MSG, SEND_B, 1, F)

    def clip(c, carry):
        here = pl.ds(pl.multiple_of(c * PT, PT), PT)
        for h in range(HEADS // 2):
            cols = slice(h * HS, (h + 1) * HS)
            q, k, v, u = q_ref[here, cols], k_ref[here, cols], v_ref[here, cols], up[here, cols]
            p = probs_of(q, k, scale, None)
            att[here, cols], dv_ref[here, cols], dq_ref[here, cols], dk_ref[here, cols] = attend(
                p, q, k, v, u, scale
            )
        return carry

    lax.fori_loop(0, 2, clip, 0)

    def grad_core(h, stage):
        moved = dot(att[...], att_m[...], 1, 0).astype(BF)
        part[h] = dot(moved, cot_ref[...], 0, 0).astype(BF)
        put(part.at[h, :, pl.ds(other_win, WIN)], rc.at[h], stage, sibling)

    def grad_x(h, stage):
        arrived(rc.at[h], stage)
        xs[h] = (part[h, :, pl.ds(win, WIN)].astype(F32) + rc[h].astype(F32)).astype(BF)
        for i in range(1, 4):
            to = lax.rem(x + i, 4)
            put(xs.at[h, rows16(to, 80)], rx.at[h, x], stage + 1, on_x(i))
        rx[h, x] = xs[h, rows16(x, 80), :]

    def total(ref, h):
        t = ref[h, 0].astype(F32)
        for i in range(1, 4):
            t = t + ref[h, i].astype(F32)
        return t

    def grad_y(h, stage):
        arrived(rx.at[h, 0:3], stage + 1)
        ys[h] = move(gx_m[...], total(rx, h).astype(BF))
        for i in range(1, 4):
            to = lax.rem(y + i, 4)
            put(ys.at[h, rows16(to, 32)], ry.at[h, y], stage + 2, on_y(i))
        ry[h, y] = ys[h, rows16(y, 32), :]

    def grad_sum(h, stage):
        arrived(ry.at[h, 0:3], stage + 2)
        zs[32 * h : 32 * (h + 1), :] = total(ry, h).astype(BF)

    grad_core(0, G_C0)

    mine = pltpu.make_async_copy(
        msg.at[lax.rem(me, 2), rows16(lax.div(me, 2))], got.at[rows16(me)], recv.at[OWN]
    )
    mine.start()
    mine.wait()
    arrived(got.at[0 : 16 * (F - 1), 0:CUT], SEND_A)

    def regroup(lo, hi):
        def body(c, carry):
            t = move(rows_m[...], got[rows16(c, 256), lo:hi])
            for g in range(4):
                grp[g, rows16(c, 64), lo:hi] = t[64 * g : 64 * (g + 1), :]
            return carry

        lax.fori_loop(0, 4, body, 0)

    keep = lax.rem(lax.broadcasted_iota(jnp.int32, (256, 256), 0), 4) == lax.rem(
        lax.broadcasted_iota(jnp.int32, (256, 256), 1), 4
    )

    regroup(0, CUT)

    def group_probs(g, carry):
        for b in range(2):
            q = grp[g, :, b * HS : (b + 1) * HS]
            k = grp[g, :, PAIR + b * HS : PAIR + (b + 1) * HS]
            prob[g, b] = probs_of(q, k, scale, keep)
        return carry

    lax.fori_loop(0, 4, group_probs, 0)

    grad_x(0, G_C0)

    arrived(got.at[0 : 16 * (F - 1), CUT:MSG], SEND_B)
    regroup(CUT, MSG)

    def group_grads(g, carry):
        for b in range(2):
            def cols(n):
                return slice(n * PAIR + b * HS, n * PAIR + (b + 1) * HS)

            q, k, v, u = (grp[g, :, cols(n)] for n in range(4))
            got_all = attend(prob[g, b], q, k, v, u, scale)
            for n in range(4):
                res[g, :, cols(n)] = got_all[n]
        return carry

    res[:, :, HW:MSG] = jnp.zeros((4, 256, MSG - HW), BF)
    lax.fori_loop(0, 4, group_grads, 0)

    def ungroup(c, carry):
        t = jnp.concatenate([res[g, rows16(c, 64), :] for g in range(4)], axis=0)
        out_msg[rows16(c, 256), :] = dot(rows_m[...], t, 0, 0).astype(BF)
        return carry

    lax.fori_loop(0, 4, ungroup, 0)

    def send_back(lo, hi, stage):
        def body(i, c):
            p = lax.rem(me + i, F)
            put(
                out_msg.at[rows16(p), lo:hi],
                back.at[lax.rem(me, 2), rows16(lax.div(me, 2)), lo:hi],
                stage,
                frame(p),
            )
            return c

        lax.fori_loop(1, F, body, 0)

    send_back(0, BACK, BACK_A)
    send_back(BACK, MSG, BACK_B)
    mine = pltpu.make_async_copy(
        out_msg.at[rows16(me)], back.at[lax.rem(me, 2), rows16(lax.div(me, 2))], recv.at[OWN]
    )
    mine.start()
    mine.wait()

    grad_y(0, G_C0)

    arrived(got.at[0 : 16 * (F - 1), 0:BACK], BACK_A)
    for hp in range(2):
        att[:, hp * PAIR : (hp + 1) * PAIR] = back[hp, :, 0:PAIR]
    grad_core(1, G_C1)
    grad_sum(0, G_C0)
    grad_x(1, G_C1)
    grad_y(1, G_C1)
    grad_sum(1, G_C1)

    zp[...] = move(gy_m[...], zs[...])
    for i in range(1, 4):
        put(zp.at[rows16(lax.rem(z + i, 4))], rz.at[0, z], G_Z, on_z(i))
    rz[0, z] = zp[rows16(z), :]
    arrived(rz.at[0, 0:3], G_Z)
    rh[0, zhi] = total(rz, 0)
    for i in range(1, 4):
        put(rh.at[0, zhi], rh.at[0, zhi], G_H, on_zhi(i))
    arrived(rh.at[0, 0:3], G_H)
    fw[:, pl.ds(win, WIN)] = total(rh, 0)
    put(fw.at[:, pl.ds(give, OFF)], fw.at[:, pl.ds(give, OFF)], G_F, sibling)

    arrived(got.at[0 : 16 * (F - 1), BACK:MSG], BACK_B)
    for hp in range(2):
        cols = slice(SIDE + PAIR * hp, SIDE + PAIR * (hp + 1))
        dv_ref[:, cols] = back[hp, :, PAIR : 2 * PAIR]
        dq_ref[:, cols] = back[hp, :, 2 * PAIR : 3 * PAIR]
        dk_ref[:, cols] = back[hp, :, 3 * PAIR : HW]

    arrived(fw.at[:, 0:OFF], G_F)
    wg_ref[...] = (fw[0:SHARE, :] * (1.0 / math.sqrt(ROWS * F * 8))).astype(BF)

    sent(g1.at[0:48], W_Z)
    sent(g2.at[0:144], W_Y)
    sent(wall.at[0:432, 0:WIN], W_X)
    sent(wall.at[:, 0:OFF], W_C)
    sent(got.at[0 : 16 * (F - 1), 0:CUT], SEND_A)
    sent(got.at[0 : 16 * (F - 1), CUT:MSG], SEND_B)
    sent(got.at[0 : 16 * (F - 1), 0:BACK], BACK_A)
    sent(got.at[0 : 16 * (F - 1), BACK:MSG], BACK_B)
    for h, stage in ((0, G_C0), (1, G_C1)):
        sent(rc.at[h], stage)
        sent(rx.at[h, 0:3], stage + 1)
        sent(ry.at[h, 0:3], stage + 2)
    sent(rz.at[0, 0:3], G_Z)
    sent(rh.at[0, 0:3], G_H)
    sent(fw.at[:, 0:OFF], G_F)


def on_device(queries, key_vectors, values, w_out, cotangent):
    tables = [
        jnp.asarray(m(), BF)
        for m in (group_rows, w_after_z, w_after_y, upstream_columns, attended_columns, grad_after_x, grad_after_y)
    ]
    vmem = pl.BlockSpec(memory_space=pltpu.VMEM)
    side = jax.ShapeDtypeStruct((ROWS, HW), BF)
    scratch = [
        ((16, WIN), BF),
        ((64, WIN), BF),
        ((48, WIN), BF),
        ((192, WIN), BF),
        ((144, WIN), BF),
        ((HW, D), BF),
        ((ROWS, HW), BF),
        ((2, ROWS, MSG), BF),
        ((16 * F, MSG), BF),
        ((4, 256, MSG), BF),
        ((4, 2, 256, 256), F32),
        ((4, 256, MSG), BF),
        ((16 * F, MSG), BF),
        ((2, ROWS, MSG), BF),
        ((ROWS, SIDE), BF),
        ((2, 320, D), BF),
        ((2, 320, WIN), BF),
        ((2, 320, WIN), BF),
        ((2, 4, 80, WIN), BF),
        ((2, 128, WIN), BF),
        ((2, 4, 32, WIN), BF),
        ((64, WIN), BF),
        ((64, WIN), BF),
        ((1, 4, 16, WIN), BF),
        ((1, 4, 16, WIN), F32),
        ((16, D), F32),
    ]
    return pl.pallas_call(
        kernel,
        out_shape=(side, side, side, jax.ShapeDtypeStruct((SHARE, D), BF)),
        in_specs=[vmem] * 12,
        out_specs=(vmem,) * 4,
        scratch_shapes=[pltpu.VMEM(s, t) for s, t in scratch]
        + [pltpu.SemaphoreType.DMA((STAGES,)), pltpu.SemaphoreType.DMA((STAGES,))],
        compiler_params=pltpu.CompilerParams(
            collective_id=0, has_side_effects=True, vmem_limit_bytes=56 * 1024 * 1024
        ),
        cost_estimate=pl.CostEstimate(flops=4_000_000_000, bytes_accessed=6_000_000, transcendentals=2_000_000),
    )(queries, key_vectors, values, w_out, cotangent, *tables)


def solution(mesh):
    rows = P(("dp", "frame"), None)
    return jax.shard_map(
        on_device,
        mesh=mesh,
        in_specs=(rows, rows, rows, P("frame", None), rows),
        out_specs=(rows, rows, rows, P("frame", None)),
        check_vma=False,
    )
```

```python
import math

import jax
import jax.numpy as jnp
import numpy as np
from jax import lax
from jax.experimental import pallas as pl
from jax.experimental.pallas import tpu as pltpu
from jax.sharding import PartitionSpec as P

HS = 72
HEADS = 8
PT = 256
D = 1152
HW = 576
ROWS = 512
SIDE = 288
PAIR = 144
MSG = 640
CUT1, CUT2 = 384, 512
BACK = 256
WIN = 640
OFF = 512
SHARE = 9
F = 64
MESH = pl.DeviceIdType.MESH
BF = jnp.bfloat16
F32 = jnp.float32

(
    W_Z, W_Y0, W_X0, W_C0, W_Y1, W_X1, W_C1, SEND_A, SEND_B, SEND_C, BACK_A, BACK_B,
    G_C0, G_X0, G_Y0, G_C1, G_X1, G_Y1, G_Z, G_H, G_F, OWN, LOAD,
) = range(23)
STAGES = 40

ATT, DV, DQ, DK = (0, 72), (144, 360), (216, 432), (288, 504)


def group_rows():
    m = np.zeros((256, 256), np.float32)
    for g in range(4):
        for f in range(16):
            for s in range(4):
                m[64 * g + 4 * f + s, 16 * f + 4 * g + s] = 1
    return m


def side_rows():
    m = np.zeros((320, SIDE), np.float32)
    for x in range(4):
        for y in range(4):
            for zz in range(2):
                for i in range(SHARE):
                    m[x * 80 + y * 18 + zz * 9 + i, (zz * 16 + y * 4 + x) * 9 + i] = 1
    return m


def spread_y():
    m = np.zeros((128, 80), np.float32)
    for y in range(4):
        for r in range(18):
            m[y * 32 + r, y * 18 + r] = 1
    return m


def spread_z():
    m = np.zeros((64, 64), np.float32)
    for h in range(2):
        for zz in range(2):
            for i in range(SHARE):
                m[(2 * h + zz) * 16 + i, h * 32 + zz * 9 + i] = 1
    return m


def dot(a, b, ca, cb):
    return lax.dot_general(a, b, (((ca,), (cb,)), ((), ())), preferred_element_type=F32)


def move(m, a):
    return dot(m, a, 1, 0).astype(BF)


def softmax_down(s, keep):
    if keep is not None:
        s = jnp.where(keep, s, -1e30)
    e = jnp.exp(s - jnp.max(s, axis=0, keepdims=True))
    return e / jnp.sum(e, axis=0, keepdims=True)


def score_grads(p, dp):
    return (p * (dp - jnp.sum(p * dp, axis=0, keepdims=True))).astype(BF)


def kernel(
    q_hbm, k_hbm, v_hbm, w_ref, cot_hbm,
    rows_m, side_m, side_t, gx_m, gx_t, gy_m, gy_t,
    dq_hbm, dk_hbm, dv_hbm, wg_ref,
    q_ref, k_ref, v_ref, cot_ref, dq_ref, dk_ref, dv_ref,
    wpad, g1, c1, g2, c2, wall, up, msg_t, msg, got, grp, prob, sprob, res, out_msg, back,
    att, part, rc, xs, rx, ys, ry, zs, zp, rz, rh, fw,
    send, recv,
):
    me, d = lax.axis_index("frame"), lax.axis_index("dp")
    core, zhi = lax.rem(d, 2), lax.div(d, 2)
    x, y, z = lax.rem(me, 4), lax.rem(lax.div(me, 4), 4), lax.div(me, 16)
    me_hp, me_row = lax.rem(me, 2), lax.div(me, 2)
    scale = 1.0 / math.sqrt(HS)
    win = pl.multiple_of(core * OFF, 128)
    other_win = pl.multiple_of((1 - core) * OFF, 128)
    give = pl.multiple_of(core * WIN, 128)

    def rows16(i, n=16):
        return pl.ds(pl.multiple_of(i * n, 16), n)

    def frame(p):
        return {"frame": p}

    def on_x(i):
        return frame(me - x + lax.rem(x + i, 4))

    def on_y(i):
        return frame(me + 4 * (lax.rem(y + i, 4) - y))

    def on_z(i):
        return frame(me + 16 * (lax.rem(z + i, 4) - z))

    def on_zhi(i):
        return {"dp": lax.rem(d + 2 * i, 8)}

    sibling = {"dp": d + 1 - 2 * core}

    def put(src, dst, stage, to):
        pltpu.make_async_remote_copy(
            src_ref=src, dst_ref=dst, send_sem=send.at[stage], recv_sem=recv.at[stage],
            device_id=to, device_id_type=MESH,
        ).start()

    def arrived(ref, stage):
        pltpu.make_async_copy(ref, ref, recv.at[stage]).wait()

    def sent(ref, stage):
        pltpu.make_async_copy(ref, ref, send.at[stage]).wait()

    barrier = pltpu.get_barrier_semaphore()

    def greet(i, c):
        pl.semaphore_signal(barrier, inc=1, device_id=frame(lax.rem(me + i, F)), device_id_type=MESH)
        return c

    lax.fori_loop(1, F, greet, 0)
    for i in range(1, 4):
        pl.semaphore_signal(barrier, inc=1, device_id=on_zhi(i), device_id_type=MESH)
    pl.semaphore_signal(barrier, inc=1, device_id=sibling, device_id_type=MESH)

    tops, bottoms = slice(0, SIDE), slice(SIDE, HW)
    loads = []
    for n, (src, dst, part_rows) in enumerate(
        [(a, b, bottoms) for a, b in ((q_hbm, q_ref), (k_hbm, k_ref), (v_hbm, v_ref))]
        + [(a, b, tops) for a, b in ((q_hbm, q_ref), (k_hbm, k_ref), (v_hbm, v_ref))]
        + [(cot_hbm, cot_ref, slice(0, ROWS))]
    ):
        loads.append(pltpu.make_async_copy(src.at[part_rows], dst.at[part_rows], recv.at[LOAD + n]))
        loads[-1].start()

    wpad[...] = jnp.zeros_like(wpad)
    wpad[0:SHARE, :] = w_ref[:, pl.ds(win, WIN)]
    msg_t[:, HW:MSG, :] = jnp.zeros((2, MSG - HW, ROWS), BF)
    for n in range(3):
        loads[n].wait()
    for hp in range(2):
        rows = slice(SIDE + PAIR * hp, SIDE + PAIR * (hp + 1))
        for n, ref in enumerate((q_ref, k_ref, v_ref)):
            msg_t[hp, n * PAIR : (n + 1) * PAIR, :] = ref[rows, :]
        msg[hp, :, 0:CUT1] = msg_t[hp, 0:CUT1, :].T

    pl.semaphore_wait(barrier, F - 1 + 4)

    for i in range(1, 4):
        put(wpad, g1.at[rows16(z)], W_Z, on_z(i))
    g1[rows16(z), :] = wpad[...]

    def send_messages(lo, hi, stage, first, last):
        def to(row, hp):
            put(msg.at[hp, rows16(row), lo:hi], got.at[rows16(me), lo:hi], stage, frame(2 * row + hp))

        def body(i, c):
            row = lax.rem(me_row + i, F // 2)
            to(row, 0)
            to(row, 1)
            return c

        if first == 0:
            to(me_row, 1 - me_hp)
            first = 1
        lax.fori_loop(first, last, body, 0)

    def w_y(h):
        for i in range(1, 4):
            put(c1.at[32 * h : 32 * (h + 1)], g2.at[h, rows16(y, 32)], W_Y0 + 3 * h, on_y(i))
        g2[h, rows16(y, 32), :] = c1[32 * h : 32 * (h + 1), :]

    def w_x(h):
        arrived(g2.at[h, 0:96], W_Y0 + 3 * h)
        c2[h] = move(gx_t[...], g2[h])
        for i in range(1, 4):
            put(c2.at[h], wall.at[h, rows16(x, 80), pl.ds(win, WIN)], W_X0 + 3 * h, on_x(i))
        wall[h, rows16(x, 80), pl.ds(win, WIN)] = c2[h]

    def w_core(h):
        arrived(wall.at[h, 0:240, 0:WIN], W_X0 + 3 * h)
        both = wall.at[h, :, pl.ds(give, OFF)]
        put(both, both, W_C0 + 3 * h, sibling)

    def upstream(h):
        arrived(wall.at[h, :, 0:OFF], W_C0 + 3 * h)
        u = dot(wall[h], cot_ref[...], 1, 1).astype(BF)
        return move(side_t[...], u)

    send_messages(0, CUT1, SEND_A, 0, 11)
    arrived(g1.at[0:48], W_Z)
    c1[...] = move(gy_t[...], g1[...])
    w_y(1)
    w_y(0)
    send_messages(0, CUT1, SEND_A, 11, 21)
    w_x(1)
    w_x(0)
    send_messages(0, CUT1, SEND_A, 21, F // 2)
    for n in range(3, 7):
        loads[n].wait()

    def clip_columns(c):
        return pl.ds(pl.multiple_of(c * PT, PT), PT)

    def head_rows(h):
        return slice(h * HS, (h + 1) * HS)

    def clip_forward(c, carry):
        here = clip_columns(c)
        for h in range(HEADS // 2):
            rows = head_rows(h)
            p = softmax_down(dot(k_ref[rows, here], q_ref[rows, here], 0, 0) * scale, None)
            sprob[c, h] = p
            att[rows, here] = dot(v_ref[rows, here], p.astype(BF), 1, 0).astype(BF)
        return carry

    def clip_backward(c, carry):
        here = clip_columns(c)
        for h in range(HEADS // 2):
            rows = head_rows(h)
            q, k, v, u = q_ref[rows, here], k_ref[rows, here], v_ref[rows, here], up[rows, here]
            p = sprob[c, h]
            dv_ref[rows, here] = dot(u, p.astype(BF), 1, 1).astype(BF)
            ds = score_grads(p, dot(v, u, 0, 0))
            dq_ref[rows, here] = (dot(k, ds, 1, 0) * scale).astype(BF)
            dk_ref[rows, here] = (dot(q, ds, 1, 1) * scale).astype(BF)
        return carry

    def grad_core(h, moved, stage):
        part[h] = dot(moved.astype(BF), cot_ref[...], 1, 0).astype(BF)
        put(part.at[h, :, pl.ds(other_win, WIN)], rc.at[h], stage, sibling)

    def grad_x(h, stage):
        arrived(rc.at[h], stage)
        xs[h] = (part[h, :, pl.ds(win, WIN)].astype(F32) + rc[h].astype(F32)).astype(BF)
        for i in range(1, 4):
            put(xs.at[h, rows16(lax.rem(x + i, 4), 80)], rx.at[h, x], stage + 1, on_x(i))
        rx[h, x] = xs[h, rows16(x, 80), :]

    def total(ref, h):
        t = ref[h, 0].astype(F32)
        for i in range(1, 4):
            t = t + ref[h, i].astype(F32)
        return t

    def grad_y(h, stage):
        arrived(rx.at[h, 0:3], stage + 1)
        ys[h] = move(gx_m[...], total(rx, h).astype(BF))
        for i in range(1, 4):
            put(ys.at[h, rows16(lax.rem(y + i, 4), 32)], ry.at[h, y], stage + 2, on_y(i))
        ry[h, y] = ys[h, rows16(y, 32), :]

    def grad_sum(h, stage):
        arrived(ry.at[h, 0:3], stage + 2)
        zs[32 * h : 32 * (h + 1), :] = total(ry, h).astype(BF)

    lax.fori_loop(0, 2, clip_forward, 0)
    w_core(1)
    grad_core(0, dot(side_m[...], att[...], 1, 0), G_C0)

    msg_t_up = upstream(1)
    for hp in range(2):
        msg_t[hp, 3 * PAIR : HW, :] = msg_t_up[hp * PAIR : (hp + 1) * PAIR, :]
        msg[hp, :, CUT1:MSG] = msg_t[hp, CUT1:MSG, :].T
    send_messages(CUT1, CUT2, SEND_B, 0, F // 2)
    w_core(0)
    send_messages(CUT2, MSG, SEND_C, 0, F // 2)

    mine = pltpu.make_async_copy(msg.at[me_hp, rows16(me_row)], got.at[rows16(me)], recv.at[OWN])
    mine.start()
    mine.wait()

    def regroup(lo, hi):
        def body(c, carry):
            t = move(rows_m[...], got[rows16(c, 256), lo:hi])
            for g in range(4):
                grp[g, rows16(c, 64), lo:hi] = t[64 * g : 64 * (g + 1), :]
            return carry

        lax.fori_loop(0, 4, body, 0)

    def ungroup(lo, hi):
        def body(c, carry):
            t = jnp.concatenate([res[g, rows16(c, 64), lo:hi] for g in range(4)], axis=0)
            out_msg[rows16(c, 256), lo:hi] = dot(rows_m[...], t, 0, 0).astype(BF)
            return carry

        lax.fori_loop(0, 4, body, 0)

    def send_back(lo, hi, stage, first, last):
        def to(row, hp):
            p = 2 * row + hp
            put(out_msg.at[rows16(p), lo:hi], back.at[me_hp, rows16(me_row), lo:hi], stage, frame(p))

        def body(i, c):
            row = lax.rem(me_row + i, F // 2)
            to(row, 0)
            to(row, 1)
            return c

        if first == 0:
            to(me_row, 1 - me_hp)
            first = 1
        lax.fori_loop(first, last, body, 0)

    keep = lax.rem(lax.broadcasted_iota(jnp.int32, (256, 256), 0), 4) == lax.rem(
        lax.broadcasted_iota(jnp.int32, (256, 256), 1), 4
    )

    def part_of(g, n, b):
        return grp[g, :, n * PAIR + b * HS : n * PAIR + (b + 1) * HS]

    def group_probs(g, carry):
        for b in range(2):
            prob[g, b] = softmax_down(dot(part_of(g, 1, b), part_of(g, 0, b), 1, 1) * scale, keep)
        return carry

    def group_attended(g, carry):
        for b in range(2):
            res[g, :, ATT[b] : ATT[b] + HS] = dot(prob[g, b].astype(BF), part_of(g, 2, b), 0, 0).astype(BF)
        return carry

    def group_grads(b):
        def body(g, carry):
            q, k, v, u = (part_of(g, n, b) for n in range(4))
            p = prob[g, b]
            res[g, :, DV[b] : DV[b] + HS] = dot(p.astype(BF), u, 1, 0).astype(BF)
            ds = score_grads(p, dot(v, u, 1, 1))
            res[g, :, DQ[b] : DQ[b] + HS] = (dot(ds, k, 0, 0) * scale).astype(BF)
            res[g, :, DK[b] : DK[b] + HS] = (dot(ds, q, 1, 0) * scale).astype(BF)
            return carry

        lax.fori_loop(0, 4, body, 0)

    res[:, :, HW:MSG] = jnp.zeros((4, 256, MSG - HW), BF)
    arrived(got.at[0 : 16 * (F - 1), 0:CUT1], SEND_A)
    regroup(0, CUT1)
    lax.fori_loop(0, 4, group_probs, 0)
    grad_x(0, G_C0)

    arrived(got.at[0 : 16 * (F - 1), CUT1:CUT2], SEND_B)
    regroup(CUT1, CUT2)
    lax.fori_loop(0, 4, group_attended, 0)
    group_grads(0)
    ungroup(0, BACK)
    send_back(0, BACK, BACK_A, 0, F // 2)

    arrived(got.at[0 : 16 * (F - 1), CUT2:MSG], SEND_C)
    regroup(CUT2, MSG)
    group_grads(1)
    ungroup(BACK, MSG)
    mine = pltpu.make_async_copy(out_msg.at[rows16(me)], back.at[me_hp, rows16(me_row)], recv.at[OWN])
    mine.start()
    mine.wait()

    grad_y(0, G_C0)
    up[...] = upstream(0)
    clip_backward(0, 0)

    sent(got.at[0 : 16 * (F - 1), 0:BACK], BACK_A)
    send_back(BACK, MSG, BACK_B, 0, 11)
    arrived(got.at[0 : 16 * (F - 1), 0:BACK], BACK_A)
    grad_core(
        1,
        dot(side_m[:, 0:PAIR], back[0, :, 0:PAIR], 1, 1) + dot(side_m[:, PAIR:SIDE], back[1, :, 0:PAIR], 1, 1),
        G_C1,
    )
    send_back(BACK, MSG, BACK_B, 11, 21)
    grad_sum(0, G_C0)
    grad_x(1, G_C1)
    send_back(BACK, MSG, BACK_B, 21, F // 2)
    clip_backward(1, 0)
    grad_y(1, G_C1)
    stores = []
    for n, (src, dst) in enumerate(((dq_ref, dq_hbm), (dk_ref, dk_hbm), (dv_ref, dv_hbm))):
        stores.append(pltpu.make_async_copy(src.at[tops], dst.at[tops], recv.at[LOAD + 7 + n]))
        stores[-1].start()
    grad_sum(1, G_C1)

    zp[...] = move(gy_m[...], zs[...])
    for i in range(1, 4):
        put(zp.at[rows16(lax.rem(z + i, 4))], rz.at[0, z], G_Z, on_z(i))
    rz[0, z] = zp[rows16(z), :]
    arrived(rz.at[0, 0:3], G_Z)
    rh[0, zhi] = total(rz, 0).astype(BF)
    for i in range(1, 4):
        put(rh.at[0, zhi], rh.at[0, zhi], G_H, on_zhi(i))

    arrived(got.at[0 : 16 * (F - 1), BACK:MSG], BACK_B)
    for hp in range(2):
        t = back[hp, :, 128:MSG].T
        for b in range(2):
            first = SIDE + PAIR * hp + HS * b
            for ref, at in ((dv_ref, DV), (dq_ref, DQ), (dk_ref, DK)):
                ref[first : first + HS, :] = t[at[b] - 128 : at[b] - 128 + HS, :]
    for n, (src, dst) in enumerate(((dq_ref, dq_hbm), (dk_ref, dk_hbm), (dv_ref, dv_hbm))):
        stores.append(pltpu.make_async_copy(src.at[bottoms], dst.at[bottoms], recv.at[LOAD + 10 + n]))
        stores[-1].start()

    arrived(rh.at[0, 0:3], G_H)
    fw[:, pl.ds(win, WIN)] = total(rh, 0)
    both = fw.at[:, pl.ds(give, OFF)]
    put(both, both, G_F, sibling)
    arrived(fw.at[:, 0:OFF], G_F)
    wg_ref[...] = (fw[0:SHARE, :] * (1.0 / math.sqrt(ROWS * F * 8))).astype(BF)

    sent(g1.at[0:48], W_Z)
    for h in range(2):
        sent(g2.at[h, 0:96], W_Y0 + 3 * h)
        sent(wall.at[h, 0:240, 0:WIN], W_X0 + 3 * h)
        sent(wall.at[h, :, 0:OFF], W_C0 + 3 * h)
    sent(got.at[0 : 16 * (F - 1), 0:CUT1], SEND_A)
    sent(got.at[0 : 16 * (F - 1), CUT1:CUT2], SEND_B)
    sent(got.at[0 : 16 * (F - 1), CUT2:MSG], SEND_C)
    sent(got.at[0 : 16 * (F - 1), BACK:MSG], BACK_B)
    for h, stage in ((0, G_C0), (1, G_C1)):
        sent(rc.at[h], stage)
        sent(rx.at[h, 0:3], stage + 1)
        sent(ry.at[h, 0:3], stage + 2)
    sent(rz.at[0, 0:3], G_Z)
    sent(rh.at[0, 0:3], G_H)
    sent(fw.at[:, 0:OFF], G_F)
    for copy in stores:
        copy.wait()


def on_device(queries, key_vectors, values, w_out, cotangent):
    tables = [
        jnp.asarray(m, BF)
        for m in (
            group_rows(), side_rows(), side_rows().T, spread_y(), spread_y().T, spread_z(), spread_z().T,
        )
    ]
    vmem, hbm = pl.BlockSpec(memory_space=pltpu.VMEM), pl.BlockSpec(memory_space=pl.ANY)
    turned = jax.ShapeDtypeStruct((HW, ROWS), BF)
    scratch = (
        [((HW, ROWS), BF)] * 3
        + [((ROWS, D), BF)]
        + [((HW, ROWS), BF)] * 3
        + [
            ((16, WIN), BF),
            ((64, WIN), BF),
            ((64, WIN), BF),
            ((2, 128, WIN), BF),
            ((2, 80, WIN), BF),
            ((2, 320, D), BF),
            ((SIDE, ROWS), BF),
            ((2, MSG, ROWS), BF),
            ((2, ROWS, MSG), BF),
            ((16 * F, MSG), BF),
            ((4, 256, MSG), BF),
            ((4, 2, 256, 256), F32),
            ((2, 4, 256, 256), F32),
            ((4, 256, MSG), BF),
            ((16 * F, MSG), BF),
            ((2, ROWS, MSG), BF),
            ((SIDE, ROWS), BF),
            ((2, 320, D), BF),
            ((2, 320, WIN), BF),
            ((2, 320, WIN), BF),
            ((2, 4, 80, WIN), BF),
            ((2, 128, WIN), BF),
            ((2, 4, 32, WIN), BF),
            ((64, WIN), BF),
            ((64, WIN), BF),
            ((1, 4, 16, WIN), BF),
            ((1, 4, 16, WIN), BF),
            ((16, D), F32),
        ]
    )
    dq, dk, dv, wg = pl.pallas_call(
        kernel,
        out_shape=(turned, turned, turned, jax.ShapeDtypeStruct((SHARE, D), BF)),
        in_specs=[hbm] * 3 + [vmem, hbm] + [vmem] * 7,
        out_specs=(hbm, hbm, hbm, vmem),
        scratch_shapes=[pltpu.VMEM(s, t) for s, t in scratch]
        + [pltpu.SemaphoreType.DMA((STAGES,)), pltpu.SemaphoreType.DMA((STAGES,))],
        compiler_params=pltpu.CompilerParams(
            collective_id=0, has_side_effects=True, vmem_limit_bytes=56 * 1024 * 1024
        ),
        cost_estimate=pl.CostEstimate(flops=4_000_000_000, bytes_accessed=6_000_000, transcendentals=2_000_000),
    )(queries.T, key_vectors.T, values.T, w_out, cotangent, *tables)
    return dq.T, dk.T, dv.T, wg


def solution(mesh):
    rows = P(("dp", "frame"), None)
    return jax.shard_map(
        on_device,
        mesh=mesh,
        in_specs=(rows, rows, rows, P("frame", None), rows),
        out_specs=(rows, rows, rows, P("frame", None)),
        check_vma=False,
    )
```

```python
import math

import jax
import jax.numpy as jnp
import numpy as np
from jax import lax
from jax.experimental import pallas as pl
from jax.experimental.pallas import tpu as pltpu
from jax.sharding import PartitionSpec as P

HS = 72
HEADS = 8
PT = 256
D = 1152
HW = 576
ROWS = 512
SIDE = 288
PAIR = 144
MSG = 640
CUT1, CUT2 = 384, 512
BACK = 256
WIN = 640
OFF = 512
SHARE = 9
F = 64
MESH = pl.DeviceIdType.MESH
BF = jnp.bfloat16
F32 = jnp.float32

(
    W_Z, W_Y0, W_X0, W_C0, W_Y1, W_X1, W_C1, SEND_A, SEND_B, SEND_C, BACK_A, BACK_B,
    G_C0, G_X0, G_Y0, G_C1, G_X1, G_Y1, G_Z0, G_Z1, G_H, G_F, OWN, LOAD,
) = range(24)
STAGES = 40

ATT, DV, DQ, DK = (0, 72), (144, 360), (216, 432), (288, 504)


def group_rows():
    m = np.zeros((256, 256), np.float32)
    for g in range(4):
        for f in range(16):
            for s in range(4):
                m[64 * g + 4 * f + s, 16 * f + 4 * g + s] = 1
    return m


def side_rows():
    m = np.zeros((320, SIDE), np.float32)
    for x in range(4):
        for y in range(4):
            for zz in range(2):
                for i in range(SHARE):
                    m[x * 80 + y * 18 + zz * 9 + i, (zz * 16 + y * 4 + x) * 9 + i] = 1
    return m


def spread_y():
    m = np.zeros((128, 80), np.float32)
    for y in range(4):
        for r in range(18):
            m[y * 32 + r, y * 18 + r] = 1
    return m


def spread_z():
    m = np.zeros((64, 64), np.float32)
    for h in range(2):
        for zz in range(2):
            for i in range(SHARE):
                m[(2 * h + zz) * 16 + i, h * 32 + zz * 9 + i] = 1
    return m


def spread_zz():
    m = np.zeros((32, 32), np.float32)
    for zz in range(2):
        for i in range(SHARE):
            m[zz * 16 + i, zz * 9 + i] = 1
    return m


def dot(a, b, ca, cb):
    return lax.dot_general(a, b, (((ca,), (cb,)), ((), ())), preferred_element_type=F32)


def move(m, a):
    return dot(m, a, 1, 0).astype(BF)


def softmax_down(s, keep):
    if keep is not None:
        s = jnp.where(keep, s, -1e30)
    e = jnp.exp(s - jnp.max(s, axis=0, keepdims=True))
    return e / jnp.sum(e, axis=0, keepdims=True)


def score_grads(p, dp):
    return (p * (dp - jnp.sum(p * dp, axis=0, keepdims=True))).astype(BF)


def kernel(
    q_hbm, k_hbm, v_hbm, w_ref, cot_hbm,
    rows_m, side_m, side_t, gx_m, gx_t, gz_m, gy_t,
    dq_hbm, dk_hbm, dv_hbm, wg_ref,
    q_ref, k_ref, v_ref, cot_ref, dq_ref, dk_ref, dv_ref,
    wpad, g1, c1, g2, c2, wall, up, msg_t, msg, got, grp, prob, sprob, res, out_msg, back,
    att, part, rc, xs, rx, ys, ry, zp, rz, rh, fw,
    send, recv,
):
    me, d = lax.axis_index("frame"), lax.axis_index("dp")
    core, zhi = lax.rem(d, 2), lax.div(d, 2)
    x, y, z = lax.rem(me, 4), lax.rem(lax.div(me, 4), 4), lax.div(me, 16)
    me_hp, me_row = lax.rem(me, 2), lax.div(me, 2)
    scale = 1.0 / math.sqrt(HS)
    win = pl.multiple_of(core * OFF, 128)
    other_win = pl.multiple_of((1 - core) * OFF, 128)
    give = pl.multiple_of(core * WIN, 128)

    def rows16(i, n=16):
        return pl.ds(pl.multiple_of(i * n, 16), n)

    def frame(p):
        return {"frame": p}

    def on_x(i):
        return frame(me - x + lax.rem(x + i, 4))

    def on_y(i):
        return frame(me + 4 * (lax.rem(y + i, 4) - y))

    def on_z(i):
        return frame(me + 16 * (lax.rem(z + i, 4) - z))

    def on_zhi(i):
        return {"dp": lax.rem(d + 2 * i, 8)}

    sibling = {"dp": d + 1 - 2 * core}

    def put(src, dst, stage, to):
        pltpu.make_async_remote_copy(
            src_ref=src, dst_ref=dst, send_sem=send.at[stage], recv_sem=recv.at[stage],
            device_id=to, device_id_type=MESH,
        ).start()

    def arrived(ref, stage):
        pltpu.make_async_copy(ref, ref, recv.at[stage]).wait()

    def sent(ref, stage):
        pltpu.make_async_copy(ref, ref, send.at[stage]).wait()

    barrier = pltpu.get_barrier_semaphore()

    def greet(i, c):
        pl.semaphore_signal(barrier, inc=1, device_id=frame(lax.rem(me + i, F)), device_id_type=MESH)
        return c

    lax.fori_loop(1, F, greet, 0)
    for i in range(1, 4):
        pl.semaphore_signal(barrier, inc=1, device_id=on_zhi(i), device_id_type=MESH)
    pl.semaphore_signal(barrier, inc=1, device_id=sibling, device_id_type=MESH)

    tops, bottoms = slice(0, SIDE), slice(SIDE, HW)
    loads = []
    for n, (src, dst, part_rows) in enumerate(
        [(a, b, bottoms) for a, b in ((q_hbm, q_ref), (k_hbm, k_ref), (v_hbm, v_ref))]
        + [(a, b, tops) for a, b in ((q_hbm, q_ref), (k_hbm, k_ref), (v_hbm, v_ref))]
        + [(cot_hbm, cot_ref, slice(0, ROWS))]
    ):
        loads.append(pltpu.make_async_copy(src.at[part_rows], dst.at[part_rows], recv.at[LOAD + n]))
        loads[-1].start()

    wpad[...] = jnp.zeros_like(wpad)
    wpad[0:SHARE, :] = w_ref[:, pl.ds(win, WIN)]
    msg_t[:, HW:MSG, :] = jnp.zeros((2, MSG - HW, ROWS), BF)
    for n in range(3):
        loads[n].wait()
    for hp in range(2):
        rows = slice(SIDE + PAIR * hp, SIDE + PAIR * (hp + 1))
        for n, ref in enumerate((q_ref, k_ref, v_ref)):
            msg_t[hp, n * PAIR : (n + 1) * PAIR, :] = ref[rows, :]
        msg[hp, :, 0:CUT1] = msg_t[hp, 0:CUT1, :].T

    pl.semaphore_wait(barrier, F - 1 + 4)

    for i in range(1, 4):
        put(wpad, g1.at[rows16(z)], W_Z, on_z(i))
    g1[rows16(z), :] = wpad[...]

    def send_messages(lo, hi, stage, first, last):
        def to(row, hp):
            put(msg.at[hp, rows16(row), lo:hi], got.at[rows16(me), lo:hi], stage, frame(2 * row + hp))

        def body(i, c):
            row = lax.rem(me_row + i, F // 2)
            to(row, 0)
            to(row, 1)
            return c

        if first == 0:
            to(me_row, 1 - me_hp)
            first = 1
        lax.fori_loop(first, last, body, 0)

    def w_y(h):
        for i in range(1, 4):
            put(c1.at[32 * h : 32 * (h + 1)], g2.at[h, rows16(y, 32)], W_Y0 + 3 * h, on_y(i))
        g2[h, rows16(y, 32), :] = c1[32 * h : 32 * (h + 1), :]

    def w_x(h):
        arrived(g2.at[h, 0:96], W_Y0 + 3 * h)
        c2[h] = move(gx_t[...], g2[h])
        for i in range(1, 4):
            put(c2.at[h], wall.at[h, rows16(x, 80), pl.ds(win, WIN)], W_X0 + 3 * h, on_x(i))
        wall[h, rows16(x, 80), pl.ds(win, WIN)] = c2[h]

    def w_core(h):
        arrived(wall.at[h, 0:240, 0:WIN], W_X0 + 3 * h)
        both = wall.at[h, :, pl.ds(give, OFF)]
        put(both, both, W_C0 + 3 * h, sibling)

    def upstream(h):
        arrived(wall.at[h, :, 0:OFF], W_C0 + 3 * h)
        u = dot(wall[h], cot_ref[...], 1, 1).astype(BF)
        return move(side_t[...], u)

    send_messages(0, CUT1, SEND_A, 0, 11)
    arrived(g1.at[0:48], W_Z)
    c1[...] = move(gy_t[...], g1[...])
    w_y(1)
    w_y(0)
    send_messages(0, CUT1, SEND_A, 11, 21)
    w_x(1)
    w_x(0)
    send_messages(0, CUT1, SEND_A, 21, F // 2)
    for n in range(3, 7):
        loads[n].wait()

    def clip_columns(c):
        return pl.ds(pl.multiple_of(c * PT, PT), PT)

    def head_rows(h):
        return slice(h * HS, (h + 1) * HS)

    def clip_forward(c, carry):
        here = clip_columns(c)
        for h in range(HEADS // 2):
            rows = head_rows(h)
            p = softmax_down(dot(k_ref[rows, here], q_ref[rows, here], 0, 0) * scale, None)
            sprob[c, h] = p
            att[rows, here] = dot(v_ref[rows, here], p.astype(BF), 1, 0).astype(BF)
        return carry

    def clip_backward(c, carry):
        here = clip_columns(c)
        for h in range(HEADS // 2):
            rows = head_rows(h)
            q, k, v, u = q_ref[rows, here], k_ref[rows, here], v_ref[rows, here], up[rows, here]
            p = sprob[c, h]
            dv_ref[rows, here] = dot(u, p.astype(BF), 1, 1).astype(BF)
            ds = score_grads(p, dot(v, u, 0, 0))
            dq_ref[rows, here] = (dot(k, ds, 1, 0) * scale).astype(BF)
            dk_ref[rows, here] = (dot(q, ds, 1, 1) * scale).astype(BF)
        return carry

    def grad_core(h, moved, stage):
        part[h] = dot(moved.astype(BF), cot_ref[...], 1, 0).astype(BF)
        put(part.at[h, :, pl.ds(other_win, WIN)], rc.at[h], stage, sibling)

    def grad_x(h, stage):
        arrived(rc.at[h], stage)
        xs[h] = (part[h, :, pl.ds(win, WIN)].astype(F32) + rc[h].astype(F32)).astype(BF)
        for i in range(1, 4):
            put(xs.at[h, rows16(lax.rem(x + i, 4), 80)], rx.at[h, x], stage + 1, on_x(i))
        rx[h, x] = xs[h, rows16(x, 80), :]

    def total(ref, h):
        t = ref[h, 0].astype(F32)
        for i in range(1, 4):
            t = t + ref[h, i].astype(F32)
        return t

    def grad_y(h, stage):
        arrived(rx.at[h, 0:3], stage + 1)
        ys[h] = move(gx_m[...], total(rx, h).astype(BF))
        for i in range(1, 4):
            put(ys.at[h, rows16(lax.rem(y + i, 4), 32)], ry.at[h, y], stage + 2, on_y(i))
        ry[h, y] = ys[h, rows16(y, 32), :]

    def grad_z(h, stage):
        arrived(ry.at[h, 0:3], stage + 2)
        zp[h] = move(gz_m[...], total(ry, h).astype(BF))
        for zz in range(2):

            @pl.when(z != 2 * h + zz)
            def _(zz=zz):
                to = frame((2 * h + zz) * 16 + y * 4 + x)
                put(zp.at[h, 16 * zz : 16 * (zz + 1)], rz.at[0, z], G_Z0 + h, to)

    def grad_h(h):
        @pl.when(lax.div(z, 2) == h)
        def _():
            rz[0, z] = zp[h, rows16(z - 2 * h), :]
            arrived(rz.at[0, 0:3], G_Z0 + h)
            rh[0, zhi] = total(rz, 0).astype(BF)
            for i in range(1, 4):
                put(rh.at[0, zhi], rh.at[0, zhi], G_H, on_zhi(i))

    lax.fori_loop(0, 2, clip_forward, 0)
    w_core(1)
    grad_core(0, dot(side_m[...], att[...], 1, 0), G_C0)

    msg_t_up = upstream(1)
    for hp in range(2):
        msg_t[hp, 3 * PAIR : HW, :] = msg_t_up[hp * PAIR : (hp + 1) * PAIR, :]
        msg[hp, :, CUT1:MSG] = msg_t[hp, CUT1:MSG, :].T
    send_messages(CUT1, CUT2, SEND_B, 0, F // 2)
    w_core(0)
    send_messages(CUT2, MSG, SEND_C, 0, F // 2)

    mine = pltpu.make_async_copy(msg.at[me_hp, rows16(me_row)], got.at[rows16(me)], recv.at[OWN])
    mine.start()
    mine.wait()

    def regroup(lo, hi):
        def body(c, carry):
            t = move(rows_m[...], got[rows16(c, 256), lo:hi])
            for g in range(4):
                grp[g, rows16(c, 64), lo:hi] = t[64 * g : 64 * (g + 1), :]
            return carry

        lax.fori_loop(0, 4, body, 0)

    def ungroup(lo, hi):
        def body(c, carry):
            t = jnp.concatenate([res[g, rows16(c, 64), lo:hi] for g in range(4)], axis=0)
            out_msg[rows16(c, 256), lo:hi] = dot(rows_m[...], t, 0, 0).astype(BF)
            return carry

        lax.fori_loop(0, 4, body, 0)

    def send_back(lo, hi, stage, first, last):
        def to(row, hp):
            p = 2 * row + hp
            put(out_msg.at[rows16(p), lo:hi], back.at[me_hp, rows16(me_row), lo:hi], stage, frame(p))

        def body(i, c):
            row = lax.rem(me_row + i, F // 2)
            to(row, 0)
            to(row, 1)
            return c

        if first == 0:
            to(me_row, 1 - me_hp)
            first = 1
        lax.fori_loop(first, last, body, 0)

    keep = lax.rem(lax.broadcasted_iota(jnp.int32, (256, 256), 0), 4) == lax.rem(
        lax.broadcasted_iota(jnp.int32, (256, 256), 1), 4
    )

    def part_of(g, n, b):
        return grp[g, :, n * PAIR + b * HS : n * PAIR + (b + 1) * HS]

    def group_probs(g, carry):
        for b in range(2):
            prob[g, b] = softmax_down(dot(part_of(g, 1, b), part_of(g, 0, b), 1, 1) * scale, keep)
        return carry

    def group_attended(g, carry):
        for b in range(2):
            res[g, :, ATT[b] : ATT[b] + HS] = dot(prob[g, b].astype(BF), part_of(g, 2, b), 0, 0).astype(BF)
        return carry

    def group_grads(b):
        def body(g, carry):
            q, k, v, u = (part_of(g, n, b) for n in range(4))
            p = prob[g, b]
            res[g, :, DV[b] : DV[b] + HS] = dot(p.astype(BF), u, 1, 0).astype(BF)
            ds = score_grads(p, dot(v, u, 1, 1))
            res[g, :, DQ[b] : DQ[b] + HS] = (dot(ds, k, 0, 0) * scale).astype(BF)
            res[g, :, DK[b] : DK[b] + HS] = (dot(ds, q, 1, 0) * scale).astype(BF)
            return carry

        lax.fori_loop(0, 4, body, 0)

    res[:, :, HW:MSG] = jnp.zeros((4, 256, MSG - HW), BF)
    arrived(got.at[0 : 16 * (F - 1), 0:CUT1], SEND_A)
    regroup(0, CUT1)
    lax.fori_loop(0, 4, group_probs, 0)
    grad_x(0, G_C0)

    arrived(got.at[0 : 16 * (F - 1), CUT1:CUT2], SEND_B)
    regroup(CUT1, CUT2)
    lax.fori_loop(0, 4, group_attended, 0)
    group_grads(0)
    ungroup(0, BACK)
    send_back(0, BACK, BACK_A, 0, F // 2)

    arrived(got.at[0 : 16 * (F - 1), CUT2:MSG], SEND_C)
    regroup(CUT2, MSG)
    group_grads(1)
    ungroup(BACK, MSG)
    mine = pltpu.make_async_copy(out_msg.at[rows16(me)], back.at[me_hp, rows16(me_row)], recv.at[OWN])
    mine.start()
    mine.wait()

    grad_y(0, G_C0)
    up[...] = upstream(0)
    clip_backward(0, 0)

    sent(got.at[0 : 16 * (F - 1), 0:BACK], BACK_A)
    send_back(BACK, MSG, BACK_B, 0, 11)
    arrived(got.at[0 : 16 * (F - 1), 0:BACK], BACK_A)
    grad_core(
        1,
        dot(side_m[:, 0:PAIR], back[0, :, 0:PAIR], 1, 1) + dot(side_m[:, PAIR:SIDE], back[1, :, 0:PAIR], 1, 1),
        G_C1,
    )
    send_back(BACK, MSG, BACK_B, 11, 21)
    grad_z(0, G_C0)
    grad_x(1, G_C1)
    send_back(BACK, MSG, BACK_B, 21, F // 2)
    clip_backward(1, 0)
    grad_y(1, G_C1)
    grad_h(0)
    stores = []
    for n, (src, dst) in enumerate(((dq_ref, dq_hbm), (dk_ref, dk_hbm), (dv_ref, dv_hbm))):
        stores.append(pltpu.make_async_copy(src.at[tops], dst.at[tops], recv.at[LOAD + 7 + n]))
        stores[-1].start()
    grad_z(1, G_C1)
    grad_h(1)

    arrived(got.at[0 : 16 * (F - 1), BACK:MSG], BACK_B)
    for hp in range(2):
        t = back[hp, :, 128:MSG].T
        for b in range(2):
            first = SIDE + PAIR * hp + HS * b
            for ref, at in ((dv_ref, DV), (dq_ref, DQ), (dk_ref, DK)):
                ref[first : first + HS, :] = t[at[b] - 128 : at[b] - 128 + HS, :]
    for n, (src, dst) in enumerate(((dq_ref, dq_hbm), (dk_ref, dk_hbm), (dv_ref, dv_hbm))):
        stores.append(pltpu.make_async_copy(src.at[bottoms], dst.at[bottoms], recv.at[LOAD + 10 + n]))
        stores[-1].start()

    arrived(rh.at[0, 0:3], G_H)
    fw[:, pl.ds(win, WIN)] = total(rh, 0)
    both = fw.at[:, pl.ds(give, OFF)]
    put(both, both, G_F, sibling)
    arrived(fw.at[:, 0:OFF], G_F)
    wg_ref[...] = (fw[0:SHARE, :] * (1.0 / math.sqrt(ROWS * F * 8))).astype(BF)

    sent(g1.at[0:48], W_Z)
    for h in range(2):
        sent(g2.at[h, 0:96], W_Y0 + 3 * h)
        sent(wall.at[h, 0:240, 0:WIN], W_X0 + 3 * h)
        sent(wall.at[h, :, 0:OFF], W_C0 + 3 * h)
    sent(got.at[0 : 16 * (F - 1), 0:CUT1], SEND_A)
    sent(got.at[0 : 16 * (F - 1), CUT1:CUT2], SEND_B)
    sent(got.at[0 : 16 * (F - 1), CUT2:MSG], SEND_C)
    sent(got.at[0 : 16 * (F - 1), BACK:MSG], BACK_B)
    for h, stage in ((0, G_C0), (1, G_C1)):
        sent(rc.at[h], stage)
        sent(rx.at[h, 0:3], stage + 1)
        sent(ry.at[h, 0:3], stage + 2)
    for h in range(2):
        pl.when(lax.div(z, 2) == h)(lambda h=h: sent(rz.at[0, 0:1], G_Z0 + h))
        pl.when(lax.div(z, 2) != h)(lambda h=h: sent(rz.at[0, 0:2], G_Z0 + h))
    sent(rh.at[0, 0:3], G_H)
    sent(fw.at[:, 0:OFF], G_F)
    for copy in stores:
        copy.wait()


def on_device(queries, key_vectors, values, w_out, cotangent):
    tables = [
        jnp.asarray(m, BF)
        for m in (
            group_rows(), side_rows(), side_rows().T, spread_y(), spread_y().T, spread_zz(), spread_z().T,
        )
    ]
    vmem, hbm = pl.BlockSpec(memory_space=pltpu.VMEM), pl.BlockSpec(memory_space=pl.ANY)
    turned = jax.ShapeDtypeStruct((HW, ROWS), BF)
    scratch = (
        [((HW, ROWS), BF)] * 3
        + [((ROWS, D), BF)]
        + [((HW, ROWS), BF)] * 3
        + [
            ((16, WIN), BF),
            ((64, WIN), BF),
            ((64, WIN), BF),
            ((2, 128, WIN), BF),
            ((2, 80, WIN), BF),
            ((2, 320, D), BF),
            ((SIDE, ROWS), BF),
            ((2, MSG, ROWS), BF),
            ((2, ROWS, MSG), BF),
            ((16 * F, MSG), BF),
            ((4, 256, MSG), BF),
            ((4, 2, 256, 256), F32),
            ((2, 4, 256, 256), F32),
            ((4, 256, MSG), BF),
            ((16 * F, MSG), BF),
            ((2, ROWS, MSG), BF),
            ((SIDE, ROWS), BF),
            ((2, 320, D), BF),
            ((2, 320, WIN), BF),
            ((2, 320, WIN), BF),
            ((2, 4, 80, WIN), BF),
            ((2, 128, WIN), BF),
            ((2, 4, 32, WIN), BF),
            ((2, 32, WIN), BF),
            ((1, 4, 16, WIN), BF),
            ((1, 4, 16, WIN), BF),
            ((16, D), F32),
        ]
    )
    dq, dk, dv, wg = pl.pallas_call(
        kernel,
        out_shape=(turned, turned, turned, jax.ShapeDtypeStruct((SHARE, D), BF)),
        in_specs=[hbm] * 3 + [vmem, hbm] + [vmem] * 7,
        out_specs=(hbm, hbm, hbm, vmem),
        scratch_shapes=[pltpu.VMEM(s, t) for s, t in scratch]
        + [pltpu.SemaphoreType.DMA((STAGES,)), pltpu.SemaphoreType.DMA((STAGES,))],
        compiler_params=pltpu.CompilerParams(
            collective_id=0, has_side_effects=True, vmem_limit_bytes=56 * 1024 * 1024
        ),
        cost_estimate=pl.CostEstimate(flops=4_000_000_000, bytes_accessed=6_000_000, transcendentals=2_000_000),
    )(queries.T, key_vectors.T, values.T, w_out, cotangent, *tables)
    return dq.T, dk.T, dv.T, wg


def solution(mesh):
    rows = P(("dp", "frame"), None)
    return jax.shard_map(
        on_device,
        mesh=mesh,
        in_specs=(rows, rows, rows, P("frame", None), rows),
        out_specs=(rows, rows, rows, P("frame", None)),
        check_vma=False,
    )
```

```python
import math

import jax
import jax.numpy as jnp
import numpy as np
from jax import lax
from jax.experimental import pallas as pl
from jax.experimental.pallas import tpu as pltpu
from jax.sharding import PartitionSpec as P

HS = 72
HEADS = 8
PT = 256
D = 1152
HW = 576
ROWS = 512
SIDE = 288
PAIR = 144
MSG = 640
CUT1, CUT2 = 384, 512
BACK = 256
WIN = 640
OFF = 512
SHARE = 9
F = 64
MESH = pl.DeviceIdType.MESH
BF = jnp.bfloat16
F32 = jnp.float32

(
    W_Z, W_Y0, W_X0, W_C0, W_Y1, W_X1, W_C1, SEND_A, SEND_B, SEND_C, BACK_A, BACK_B,
    G_C0, G_X0, G_Y0, G_C1, G_X1, G_Y1, G_Z0, G_Z1, G_H, G_F, OWN, LOAD,
) = range(24)
STAGES = 40

ATT, DV, DQ, DK = (0, 72), (144, 360), (216, 432), (288, 504)


def group_rows():
    m = np.zeros((256, 256), np.float32)
    for g in range(4):
        for f in range(16):
            for s in range(4):
                m[64 * g + 4 * f + s, 16 * f + 4 * g + s] = 1
    return m


def side_rows():
    m = np.zeros((320, SIDE), np.float32)
    for x in range(4):
        for y in range(4):
            for zz in range(2):
                for i in range(SHARE):
                    m[x * 80 + y * 18 + zz * 9 + i, (zz * 16 + y * 4 + x) * 9 + i] = 1
    return m


def spread_y():
    m = np.zeros((128, 80), np.float32)
    for y in range(4):
        for r in range(18):
            m[y * 32 + r, y * 18 + r] = 1
    return m


def spread_z():
    m = np.zeros((64, 64), np.float32)
    for h in range(2):
        for zz in range(2):
            for i in range(SHARE):
                m[(2 * h + zz) * 16 + i, h * 32 + zz * 9 + i] = 1
    return m


def spread_zz():
    m = np.zeros((32, 32), np.float32)
    for zz in range(2):
        for i in range(SHARE):
            m[zz * 16 + i, zz * 9 + i] = 1
    return m


def dot(a, b, ca, cb):
    return lax.dot_general(a, b, (((ca,), (cb,)), ((), ())), preferred_element_type=F32)


def move(m, a):
    return dot(m, a, 1, 0).astype(BF)


def softmax_down(s, keep):
    if keep is not None:
        s = jnp.where(keep, s, -1e30)
    e = jnp.exp(s - jnp.max(s, axis=0, keepdims=True))
    return e / jnp.sum(e, axis=0, keepdims=True)


def score_grads(p, dp):
    return (p * (dp - jnp.sum(p * dp, axis=0, keepdims=True))).astype(BF)


def kernel(
    q_hbm, k_hbm, v_hbm, w_ref, cot_hbm,
    rows_m, side_m, side_t, gx_m, gx_t, gz_m, gy_t,
    dq_hbm, dk_hbm, dv_hbm, wg_ref,
    q_ref, k_ref, v_ref, cot_ref, dq_ref, dk_ref, dv_ref,
    wpad, g1, c1, g2, c2, wall, up, msg_t, msg, got, grp, prob, sprob, res, out_msg, back,
    att, part, rc, xs, rx, ys, ry, zp, rz, rh, fw,
    send, recv,
):
    me, d = lax.axis_index("frame"), lax.axis_index("dp")
    core, zhi = lax.rem(d, 2), lax.div(d, 2)
    x, y, z = lax.rem(me, 4), lax.rem(lax.div(me, 4), 4), lax.div(me, 16)
    me_hp, me_row = lax.rem(me, 2), lax.div(me, 2)
    scale = 1.0 / math.sqrt(HS)
    win = pl.multiple_of(core * OFF, 128)
    other_win = pl.multiple_of((1 - core) * OFF, 128)
    give = pl.multiple_of(core * WIN, 128)

    def rows16(i, n=16):
        return pl.ds(pl.multiple_of(i * n, 16), n)

    def frame(p):
        return {"frame": p}

    def on_x(i):
        return frame(me - x + lax.rem(x + i, 4))

    def on_y(i):
        return frame(me + 4 * (lax.rem(y + i, 4) - y))

    def on_z(i):
        return frame(me + 16 * (lax.rem(z + i, 4) - z))

    def on_zhi(i):
        return {"dp": lax.rem(d + 2 * i, 8)}

    sibling = {"dp": d + 1 - 2 * core}

    def put(src, dst, stage, to):
        pltpu.make_async_remote_copy(
            src_ref=src, dst_ref=dst, send_sem=send.at[stage], recv_sem=recv.at[stage],
            device_id=to, device_id_type=MESH,
        ).start()

    def arrived(ref, stage):
        pltpu.make_async_copy(ref, ref, recv.at[stage]).wait()

    def sent(ref, stage):
        pltpu.make_async_copy(ref, ref, send.at[stage]).wait()

    barrier = pltpu.get_barrier_semaphore()

    def greet(i, c):
        pl.semaphore_signal(barrier, inc=1, device_id=frame(lax.rem(me + i, F)), device_id_type=MESH)
        return c

    lax.fori_loop(1, F, greet, 0)
    for i in range(1, 4):
        pl.semaphore_signal(barrier, inc=1, device_id=on_zhi(i), device_id_type=MESH)
    pl.semaphore_signal(barrier, inc=1, device_id=sibling, device_id_type=MESH)

    tops, bottoms = slice(0, SIDE), slice(SIDE, HW)
    loads = []
    for n, (src, dst, part_rows) in enumerate(
        [(a, b, bottoms) for a, b in ((q_hbm, q_ref), (k_hbm, k_ref), (v_hbm, v_ref))]
        + [(a, b, tops) for a, b in ((q_hbm, q_ref), (k_hbm, k_ref), (v_hbm, v_ref))]
        + [(cot_hbm, cot_ref, slice(0, ROWS))]
    ):
        loads.append(pltpu.make_async_copy(src.at[part_rows], dst.at[part_rows], recv.at[LOAD + n]))
        loads[-1].start()

    wpad[...] = jnp.zeros_like(wpad)
    wpad[0:SHARE, :] = w_ref[:, pl.ds(win, WIN)]
    msg_t[:, HW:MSG, :] = jnp.zeros((2, MSG - HW, ROWS), BF)
    for n in range(3):
        loads[n].wait()
    for hp in range(2):
        rows = slice(SIDE + PAIR * hp, SIDE + PAIR * (hp + 1))
        for n, ref in enumerate((q_ref, k_ref, v_ref)):
            msg_t[hp, n * PAIR : (n + 1) * PAIR, :] = ref[rows, :]
        msg[hp, :, 0:CUT1] = msg_t[hp, 0:CUT1, :].T

    pl.semaphore_wait(barrier, F - 1 + 4)

    for i in range(1, 4):
        put(wpad, g1.at[rows16(z)], W_Z, on_z(i))
    g1[rows16(z), :] = wpad[...]

    def send_messages(lo, hi, stage, first, last):
        def to(row, hp):
            put(msg.at[hp, rows16(row), lo:hi], got.at[rows16(me), lo:hi], stage, frame(2 * row + hp))

        def body(i, c):
            row = lax.rem(me_row + i, F // 2)
            to(row, 0)
            to(row, 1)
            return c

        if first == 0:
            to(me_row, 1 - me_hp)
            first = 1
        lax.fori_loop(first, last, body, 0)

    def w_y(h):
        for i in range(1, 4):
            put(c1.at[32 * h : 32 * (h + 1)], g2.at[h, rows16(y, 32)], W_Y0 + 3 * h, on_y(i))
        g2[h, rows16(y, 32), :] = c1[32 * h : 32 * (h + 1), :]

    def w_x(h):
        arrived(g2.at[h, 0:96], W_Y0 + 3 * h)
        c2[h] = move(gx_t[...], g2[h])
        for i in range(1, 4):
            put(c2.at[h], wall.at[h, rows16(x, 80), pl.ds(win, WIN)], W_X0 + 3 * h, on_x(i))
        wall[h, rows16(x, 80), pl.ds(win, WIN)] = c2[h]

    def w_core(h):
        arrived(wall.at[h, 0:240, 0:WIN], W_X0 + 3 * h)
        both = wall.at[h, :, pl.ds(give, OFF)]
        put(both, both, W_C0 + 3 * h, sibling)

    def upstream(h):
        arrived(wall.at[h, :, 0:OFF], W_C0 + 3 * h)
        u = dot(wall[h], cot_ref[...], 1, 1).astype(BF)
        return move(side_t[...], u)

    send_messages(0, CUT1, SEND_A, 0, 11)
    arrived(g1.at[0:48], W_Z)
    c1[...] = move(gy_t[...], g1[...])
    w_y(1)
    w_y(0)
    send_messages(0, CUT1, SEND_A, 11, 21)
    w_x(1)
    w_x(0)
    send_messages(0, CUT1, SEND_A, 21, F // 2)
    for n in range(3, 7):
        loads[n].wait()

    def clip_columns(c):
        return pl.ds(pl.multiple_of(c * PT, PT), PT)

    def head_rows(h):
        return slice(h * HS, (h + 1) * HS)

    def clip_forward(c, carry):
        here = clip_columns(c)
        for h in range(HEADS // 2):
            rows = head_rows(h)
            p = softmax_down(dot(k_ref[rows, here], q_ref[rows, here], 0, 0) * scale, None)
            sprob[c, h] = p
            att[rows, here] = dot(v_ref[rows, here], p.astype(BF), 1, 0).astype(BF)
        return carry

    def clip_backward(c, carry):
        here = clip_columns(c)
        for h in range(HEADS // 2):
            rows = head_rows(h)
            q, k, v, u = q_ref[rows, here], k_ref[rows, here], v_ref[rows, here], up[rows, here]
            p = sprob[c, h]
            dv_ref[rows, here] = dot(u, p.astype(BF), 1, 1).astype(BF)
            ds = score_grads(p, dot(v, u, 0, 0))
            dq_ref[rows, here] = (dot(k, ds, 1, 0) * scale).astype(BF)
            dk_ref[rows, here] = (dot(q, ds, 1, 1) * scale).astype(BF)
        return carry

    def grad_core(h, moved, stage):
        part[h] = dot(moved.astype(BF), cot_ref[...], 1, 0).astype(BF)
        put(part.at[h, :, pl.ds(other_win, WIN)], rc.at[h], stage, sibling)

    def grad_x(h, stage):
        arrived(rc.at[h], stage)
        xs[h] = (part[h, :, pl.ds(win, WIN)].astype(F32) + rc[h].astype(F32)).astype(BF)
        for i in range(1, 4):
            put(xs.at[h, rows16(lax.rem(x + i, 4), 80)], rx.at[h, x], stage + 1, on_x(i))
        rx[h, x] = xs[h, rows16(x, 80), :]

    def total(ref, h):
        t = ref[h, 0].astype(F32)
        for i in range(1, 4):
            t = t + ref[h, i].astype(F32)
        return t

    def grad_y(h, stage):
        arrived(rx.at[h, 0:3], stage + 1)
        ys[h] = move(gx_m[...], total(rx, h).astype(BF))
        for i in range(1, 4):
            put(ys.at[h, rows16(lax.rem(y + i, 4), 32)], ry.at[h, y], stage + 2, on_y(i))
        ry[h, y] = ys[h, rows16(y, 32), :]

    def grad_z(h, stage):
        arrived(ry.at[h, 0:3], stage + 2)
        zp[h] = move(gz_m[...], total(ry, h).astype(BF))
        for zz in range(2):

            @pl.when(z != 2 * h + zz)
            def _(zz=zz):
                to = frame((2 * h + zz) * 16 + y * 4 + x)
                put(zp.at[h, 16 * zz : 16 * (zz + 1)], rz.at[0, z], G_Z0 + h, to)

    def grad_h(h):
        @pl.when(lax.div(z, 2) == h)
        def _():
            rz[0, z] = zp[h, rows16(z - 2 * h), :]
            arrived(rz.at[0, 0:3], G_Z0 + h)
            rh[0, zhi] = total(rz, 0).astype(BF)
            for i in range(1, 4):
                put(rh.at[0, zhi], rh.at[0, zhi], G_H, on_zhi(i))

    lax.fori_loop(0, 2, clip_forward, 0)
    w_core(1)
    grad_core(0, dot(side_m[...], att[...], 1, 0), G_C0)

    msg_t_up = upstream(1)
    for hp in range(2):
        msg_t[hp, 3 * PAIR : HW, :] = msg_t_up[hp * PAIR : (hp + 1) * PAIR, :]
        msg[hp, :, CUT1:MSG] = msg_t[hp, CUT1:MSG, :].T
    send_messages(CUT1, CUT2, SEND_B, 0, F // 2)
    w_core(0)
    send_messages(CUT2, MSG, SEND_C, 0, F // 2)

    mine = pltpu.make_async_copy(msg.at[me_hp, rows16(me_row)], got.at[rows16(me)], recv.at[OWN])
    mine.start()
    mine.wait()

    def regroup(lo, hi):
        def body(c, carry):
            t = move(rows_m[...], got[rows16(c, 256), lo:hi])
            for g in range(4):
                grp[g, rows16(c, 64), lo:hi] = t[64 * g : 64 * (g + 1), :]
            return carry

        lax.fori_loop(0, 4, body, 0)

    def ungroup(lo, hi):
        def body(c, carry):
            t = jnp.concatenate([res[g, rows16(c, 64), lo:hi] for g in range(4)], axis=0)
            out_msg[rows16(c, 256), lo:hi] = dot(rows_m[...], t, 0, 0).astype(BF)
            return carry

        lax.fori_loop(0, 4, body, 0)

    def send_back(lo, hi, stage, first, last):
        def to(row, hp):
            p = 2 * row + hp
            put(out_msg.at[rows16(p), lo:hi], back.at[me_hp, rows16(me_row), lo:hi], stage, frame(p))

        def body(i, c):
            row = lax.rem(me_row + i, F // 2)
            to(row, 0)
            to(row, 1)
            return c

        if first == 0:
            to(me_row, 1 - me_hp)
            first = 1
        lax.fori_loop(first, last, body, 0)

    keep = lax.rem(lax.broadcasted_iota(jnp.int32, (256, 256), 0), 4) == lax.rem(
        lax.broadcasted_iota(jnp.int32, (256, 256), 1), 4
    )

    def part_of(g, n, b):
        return grp[g, :, n * PAIR + b * HS : n * PAIR + (b + 1) * HS]

    def group_probs(g, carry):
        for b in range(2):
            prob[g, b] = softmax_down(dot(part_of(g, 1, b), part_of(g, 0, b), 1, 1) * scale, keep)
        return carry

    def group_attended(g, carry):
        for b in range(2):
            res[g, :, ATT[b] : ATT[b] + HS] = dot(prob[g, b].astype(BF), part_of(g, 2, b), 0, 0).astype(BF)
        return carry

    def group_grads(b):
        def body(g, carry):
            q, k, v, u = (part_of(g, n, b) for n in range(4))
            p = prob[g, b]
            res[g, :, DV[b] : DV[b] + HS] = dot(p.astype(BF), u, 1, 0).astype(BF)
            ds = score_grads(p, dot(v, u, 1, 1))
            res[g, :, DQ[b] : DQ[b] + HS] = (dot(ds, k, 0, 0) * scale).astype(BF)
            res[g, :, DK[b] : DK[b] + HS] = (dot(ds, q, 1, 0) * scale).astype(BF)
            return carry

        lax.fori_loop(0, 4, body, 0)

    res[:, :, HW:MSG] = jnp.zeros((4, 256, MSG - HW), BF)
    arrived(got.at[0 : 16 * (F - 1), 0:CUT1], SEND_A)
    regroup(0, CUT1)
    lax.fori_loop(0, 4, group_probs, 0)
    grad_x(0, G_C0)

    arrived(got.at[0 : 16 * (F - 1), CUT1:CUT2], SEND_B)
    regroup(CUT1, CUT2)
    lax.fori_loop(0, 4, group_attended, 0)
    group_grads(0)
    ungroup(0, BACK)
    send_back(0, BACK, BACK_A, 0, F // 2)

    arrived(got.at[0 : 16 * (F - 1), CUT2:MSG], SEND_C)
    regroup(CUT2, MSG)
    group_grads(1)
    ungroup(BACK, MSG)
    mine = pltpu.make_async_copy(out_msg.at[rows16(me)], back.at[me_hp, rows16(me_row)], recv.at[OWN])
    mine.start()
    mine.wait()

    grad_y(0, G_C0)
    up[...] = upstream(0)
    clip_backward(0, 0)

    sent(got.at[0 : 16 * (F - 1), 0:BACK], BACK_A)
    arrived(got.at[0 : 16 * (F - 1), 0:BACK], BACK_A)
    grad_core(
        1,
        dot(side_m[:, 0:PAIR], back[0, :, 0:PAIR], 1, 1) + dot(side_m[:, PAIR:SIDE], back[1, :, 0:PAIR], 1, 1),
        G_C1,
    )
    send_back(BACK, MSG, BACK_B, 0, 18)
    grad_z(0, G_C0)
    grad_x(1, G_C1)
    send_back(BACK, MSG, BACK_B, 18, F // 2)
    clip_backward(1, 0)
    grad_y(1, G_C1)
    grad_h(0)
    stores = []
    for n, (src, dst) in enumerate(((dq_ref, dq_hbm), (dk_ref, dk_hbm), (dv_ref, dv_hbm))):
        stores.append(pltpu.make_async_copy(src.at[tops], dst.at[tops], recv.at[LOAD + 7 + n]))
        stores[-1].start()
    grad_z(1, G_C1)
    grad_h(1)

    arrived(got.at[0 : 16 * (F - 1), BACK:MSG], BACK_B)
    for hp in range(2):
        t = back[hp, :, 128:MSG].T
        for b in range(2):
            first = SIDE + PAIR * hp + HS * b
            for ref, at in ((dv_ref, DV), (dq_ref, DQ), (dk_ref, DK)):
                ref[first : first + HS, :] = t[at[b] - 128 : at[b] - 128 + HS, :]
    for n, (src, dst) in enumerate(((dq_ref, dq_hbm), (dk_ref, dk_hbm), (dv_ref, dv_hbm))):
        stores.append(pltpu.make_async_copy(src.at[bottoms], dst.at[bottoms], recv.at[LOAD + 10 + n]))
        stores[-1].start()

    arrived(rh.at[0, 0:3], G_H)
    fw[:, pl.ds(win, WIN)] = total(rh, 0)
    both = fw.at[:, pl.ds(give, OFF)]
    put(both, both, G_F, sibling)
    arrived(fw.at[:, 0:OFF], G_F)
    wg_ref[...] = (fw[0:SHARE, :] * (1.0 / math.sqrt(ROWS * F * 8))).astype(BF)

    sent(g1.at[0:48], W_Z)
    for h in range(2):
        sent(g2.at[h, 0:96], W_Y0 + 3 * h)
        sent(wall.at[h, 0:240, 0:WIN], W_X0 + 3 * h)
        sent(wall.at[h, :, 0:OFF], W_C0 + 3 * h)
    sent(got.at[0 : 16 * (F - 1), 0:CUT1], SEND_A)
    sent(got.at[0 : 16 * (F - 1), CUT1:CUT2], SEND_B)
    sent(got.at[0 : 16 * (F - 1), CUT2:MSG], SEND_C)
    sent(got.at[0 : 16 * (F - 1), BACK:MSG], BACK_B)
    for h, stage in ((0, G_C0), (1, G_C1)):
        sent(rc.at[h], stage)
        sent(rx.at[h, 0:3], stage + 1)
        sent(ry.at[h, 0:3], stage + 2)
    for h in range(2):
        pl.when(lax.div(z, 2) == h)(lambda h=h: sent(rz.at[0, 0:1], G_Z0 + h))
        pl.when(lax.div(z, 2) != h)(lambda h=h: sent(rz.at[0, 0:2], G_Z0 + h))
    sent(rh.at[0, 0:3], G_H)
    sent(fw.at[:, 0:OFF], G_F)
    for copy in stores:
        copy.wait()


def copy_out(a, b, c, d, to_a, to_b, to_c, to_d):
    for src, dst in ((a, to_a), (b, to_b), (c, to_c), (d, to_d)):
        dst[...] = src[...]


def on_device(queries, key_vectors, values, w_out, cotangent):
    tables = [
        jnp.asarray(m, BF)
        for m in (
            group_rows(), side_rows(), side_rows().T, spread_y(), spread_y().T, spread_zz(), spread_z().T,
        )
    ]
    vmem, hbm = pl.BlockSpec(memory_space=pltpu.VMEM), pl.BlockSpec(memory_space=pl.ANY)
    turned = jax.ShapeDtypeStruct((HW, ROWS), BF)
    scratch = (
        [((HW, ROWS), BF)] * 3
        + [((ROWS, D), BF)]
        + [((HW, ROWS), BF)] * 3
        + [
            ((16, WIN), BF),
            ((64, WIN), BF),
            ((64, WIN), BF),
            ((2, 128, WIN), BF),
            ((2, 80, WIN), BF),
            ((2, 320, D), BF),
            ((SIDE, ROWS), BF),
            ((2, MSG, ROWS), BF),
            ((2, ROWS, MSG), BF),
            ((16 * F, MSG), BF),
            ((4, 256, MSG), BF),
            ((4, 2, 256, 256), F32),
            ((2, 4, 256, 256), F32),
            ((4, 256, MSG), BF),
            ((16 * F, MSG), BF),
            ((2, ROWS, MSG), BF),
            ((SIDE, ROWS), BF),
            ((2, 320, D), BF),
            ((2, 320, WIN), BF),
            ((2, 320, WIN), BF),
            ((2, 4, 80, WIN), BF),
            ((2, 128, WIN), BF),
            ((2, 4, 32, WIN), BF),
            ((2, 32, WIN), BF),
            ((1, 4, 16, WIN), BF),
            ((1, 4, 16, WIN), BF),
            ((16, D), F32),
        ]
    )
    dq, dk, dv, wg = pl.pallas_call(
        kernel,
        out_shape=(turned, turned, turned, jax.ShapeDtypeStruct((SHARE, D), BF)),
        in_specs=[hbm] * 3 + [vmem, hbm] + [vmem] * 7,
        out_specs=(hbm, hbm, hbm, vmem),
        scratch_shapes=[pltpu.VMEM(s, t) for s, t in scratch]
        + [pltpu.SemaphoreType.DMA((STAGES,)), pltpu.SemaphoreType.DMA((STAGES,))],
        compiler_params=pltpu.CompilerParams(
            collective_id=0, has_side_effects=True, vmem_limit_bytes=56 * 1024 * 1024
        ),
        cost_estimate=pl.CostEstimate(flops=4_000_000_000, bytes_accessed=6_000_000, transcendentals=2_000_000),
    )(queries.T, key_vectors.T, values.T, w_out, cotangent, *tables)
    dq, dk, dv, wg = pl.pallas_call(
        copy_out,
        out_shape=(turned, turned, turned, jax.ShapeDtypeStruct((SHARE, D), BF)),
        in_specs=[vmem] * 4,
        out_specs=(vmem,) * 4,
    )(dq, dk, dv, wg)
    return dq.T, dk.T, dv.T, wg


def solution(mesh):
    rows = P(("dp", "frame"), None)
    return jax.shard_map(
        on_device,
        mesh=mesh,
        in_specs=(rows, rows, rows, P("frame", None), rows),
        out_specs=(rows, rows, rows, P("frame", None)),
        check_vma=False,
    )
```
